32 devices in a mesh: grp: 4 (over y, x), dev: 8 (over z, core).
Axes of the slice: x: 2, y: 2, z: 4, core: 2. Of those that a mesh axis runs over, the one named last changes fastest.
Arguments:
- block_vectors: float32 [16384, 64], P(('grp', 'dev')), may hold values from -6 to 6
- hamiltonian: float32 [256, 64, 2048], P(('grp', 'dev')), may hold values from -0.125 to 0.125
- pattern: int32 [256, 32], P(('grp', 'dev')), may hold values from 0 to 255, as said below
- owned_blocks: int32 [32], P(('grp', 'dev')), may hold values from 1 to 8, as said below
- spectrum: float32 [2], replicated, may hold values from 0.5 to 2
Outputs:
- basis: float32 [16384, 64], P(('grp', 'dev'))
- r_factor: float32 [64, 64], replicated
The draws below stay inside these ranges and needn't reach their ends.
Inputs may be any that keep to these rules, and one draw needn't show every extreme that they name: pattern[b, 0] = b; every other entry is b + o clipped to the slots, for a distinct nonzero o with |o| <= 16. `owned_blocks`: some device owns all 8 slots.
All inputs are finite; a program needn't handle non-finite values.
Results may differ from the reference program's by a relative error of at most 0.0003.
Values sent between devices are 32-bit elements; how exact they have to be, the bound alone decides.
No kernel may reach another device: no remote copies, remote signals or barrier semaphores. Data moves between devices by JAX's collectives and lax.ppermute only.
A program may use at most 64 MiB of HBM per device.

```python
import math
import jax
import jax.numpy as jnp
from jax import lax

BS = 64
COLS = 64
NBR = 32
BAND = 16
RB_CAP = 8
NBLK = 256
DEVICES = 32


def draw_pattern(key, part):
    key = jax.random.fold_in(key, 11)
    offsets_all = jnp.concatenate([jnp.arange(-BAND, 0, dtype=jnp.int32), jnp.arange(1, BAND + 1, dtype=jnp.int32)])
    row_keys = jax.random.split(key, NBLK)
    orders = jax.vmap(lambda single: jax.random.permutation(single, 2 * BAND))(row_keys)
    chosen = offsets_all[orders[:, :NBR - 1]]
    rows = jnp.arange(NBLK, dtype=jnp.int32)[:, None]
    others = jnp.clip(rows + chosen, 0, NBLK - 1)
    return jnp.concatenate([rows, others], axis=1).astype(jnp.int32)


def draw_owned_blocks(key, part):
    key = jax.random.fold_in(key, 23)
    key_base, key_full, key_pick = jax.random.split(key, 3)
    base = jax.random.randint(key_base, (DEVICES,), 1, max(1, RB_CAP // 2) + 1)
    full = jax.random.randint(key_full, (DEVICES,), 0, 8) == 0
    counts = jnp.where(full, RB_CAP, base)
    pick = jax.random.randint(key_pick, (), 0, DEVICES)
    counts = counts.at[pick].set(RB_CAP)
    return counts.astype(jnp.int32)


def block_levels(rng, shape, cuts, low, high):
    def one(dim, blocks):
        steps = jax.random.uniform(jax.random.fold_in(jax.random.fold_in(rng, 6), dim), (blocks,), jnp.float32, low / len(cuts), high / len(cuts))
        return jnp.repeat(jnp.exp(steps), shape[dim] // blocks).reshape((-1,) + (1,) * (len(shape) - dim - 1))

    gain = one(*cuts[0])
    for cut in cuts[1:]:
        gain = gain * one(*cut)
    return gain


def bell_draw(rng, dims, scale, bound, shards=(), kind=jnp.bfloat16):
    factor_of = block_levels(rng, dims, shards, -0.22, 0.18) if shards else 1.0
    result = jax.random.normal(rng, dims, jnp.float32) * scale * factor_of
    return jnp.minimum(jnp.maximum(result, -bound), bound).astype(kind)


def setup_inputs(seed: int = 0) -> dict:
    seeds = jax.random.split(jax.random.key(seed), 6)
    block_vectors = bell_draw(seeds[0], (NBLK * BS, COLS), 1.0, 6.0, ((0, 32),), jnp.float32)
    hamiltonian = bell_draw(seeds[1], (NBLK, BS, NBR * BS), (NBR * BS) ** -0.5, 0.125, ((0, 32),), jnp.float32)
    pattern = draw_pattern(jax.random.fold_in(seeds[5], 71), 0)
    owned_blocks = draw_owned_blocks(jax.random.fold_in(seeds[5], 71), 0)
    spectrum = jnp.clip(jnp.exp(jax.random.uniform(seeds[4], (2,), jnp.float32, math.log(0.5), math.log(2.0))), 0.5, 2.0)
    return {"block_vectors": block_vectors, "hamiltonian": hamiltonian, "pattern": pattern, "owned_blocks": owned_blocks, "spectrum": spectrum}


def apply_matrix(blocks, hamiltonian, pattern):
    groups = NBLK // RB_CAP
    mats = hamiltonian.reshape(groups, RB_CAP, BS, NBR * BS)
    pats = pattern.reshape(groups, RB_CAP, NBR)

    def one_group(pair):
        mat, pat = pair
        picked = blocks[pat].reshape(RB_CAP, NBR * BS, COLS)
        return jnp.einsum('gik,gkc->gic', mat, picked, precision=lax.Precision.HIGHEST)
    return lax.map(one_group, (mats, pats)).reshape(NBLK, BS, COLS)

def reference(block_vectors, hamiltonian, pattern, owned_blocks, spectrum):
    slots = jnp.arange(NBLK, dtype=jnp.int32)
    live = slots % RB_CAP < jnp.repeat(owned_blocks, RB_CAP)
    live_mask = live.astype(jnp.float32)[:, None, None]
    shift_value = spectrum[0]
    scale_value = spectrum[1]
    first_vec = block_vectors.reshape(NBLK, BS, COLS) * live_mask
    second_vec = live_mask * ((apply_matrix(first_vec, hamiltonian, pattern) - shift_value * first_vec) / scale_value)
    third_vec = live_mask * (2.0 * (apply_matrix(second_vec, hamiltonian, pattern) - shift_value * second_vec) / scale_value - first_vec)
    flat = third_vec.reshape(NBLK * BS, COLS)
    q_mat, r_mat = jnp.linalg.qr(flat)
    signs = jnp.sign(jnp.diagonal(r_mat))
    q_mat = q_mat * signs[None, :]
    r_mat = r_mat * signs[:, None]
    total = jnp.sqrt(jnp.float32(NBLK * BS))
    return (q_mat * total, r_mat / total)
```

```python
import functools

import jax
import jax.numpy as jnp
from jax import lax
from jax.experimental import pallas as pl
from jax.experimental.pallas import tpu as pltpu
from jax.sharding import PartitionSpec as P

BAND = 16
AXES = ("grp", "dev")
SPLITS = 3


def shifted(block, distance):
    devices = range(lax.axis_size(AXES))
    route = [(i - distance, i) for i in devices if i - distance in devices]
    return lax.ppermute(block, AXES, route)


def split_float(values):
    parts = []
    rest = values
    for _ in range(SPLITS - 1):
        part = rest.astype(jnp.bfloat16)
        parts.append(part)
        rest = rest - part.astype(jnp.float32)
    parts.append(rest.astype(jnp.bfloat16))
    return jnp.concatenate(parts, axis=0)


def joined_product(product, rows, columns):
    def part(i, j):
        return product[i * rows : (i + 1) * rows, j * columns : (j + 1) * columns]

    second = part(0, 2) + part(1, 1) + part(2, 0)
    first = part(0, 1) + part(1, 0)
    return part(0, 0) + (first + second)


def apply_kernel(
    first_apply,
    reach_dev,
    pattern_ref,
    owned_ref,
    spectrum_ref,
    *refs,
):
    sources = refs[: 2 * reach_dev + 1]
    refs = refs[2 * reach_dev + 1 :]
    if first_apply:
        matrix_ref, out_ref, held, window, product, arrived = refs
    else:
        start_ref, matrix_ref, out_ref, gram_ref, held, window, product, arrived = refs
    own_ref = sources[reach_dev]
    columns, rows = own_ref.shape
    block_count, block_size, width = held.shape
    neighbours = width // block_size

    def fetch(b):
        return pltpu.make_async_copy(matrix_ref.at[b], held.at[b], arrived.at[b])

    for b in range(block_count):
        fetch(b).start()
    for s, source in enumerate(sources):
        window[s * rows : (s + 1) * rows, :] = split_float(source[...]).T

    first_slot = reach_dev * block_count - pattern_ref[0, 0]
    chunk = 4
    for b in range(block_count):
        fetch(b).wait()
        total = None
        for c in range(0, neighbours, chunk):
            left = split_float(held[b, :, c * block_size : (c + chunk) * block_size])
            picked = []
            for k in range(c, c + chunk):
                slot = pattern_ref[b, k] + first_slot
                start = pl.multiple_of(slot * block_size, block_size)
                picked.append(window[pl.ds(start, block_size), :])
            right = jnp.concatenate(picked, axis=0)
            term = jnp.dot(left, right, preferred_element_type=jnp.float32)
            total = term if total is None else total + term
        product[b * block_size : (b + 1) * block_size, :] = joined_product(
            total, block_size, columns
        )

    live_rows = owned_ref[0] * block_size
    live = lax.broadcasted_iota(jnp.int32, (columns, rows), 1) < live_rows
    shift_value = spectrum_ref[0]
    scale_value = spectrum_ref[1]
    moved = product[...].T - shift_value * own_ref[...]
    if first_apply:
        out_ref[...] = jnp.where(live, moved / scale_value, 0.0)
    else:
        result = jnp.where(live, 2.0 * moved / scale_value - start_ref[...], 0.0)
        out_ref[...] = result
        parts = split_float(result)
        gram = lax.dot_general(
            parts, parts, (((1,), (1,)), ((), ())), preferred_element_type=jnp.float32
        )
        gram_ref[...] = joined_product(gram, columns, columns)


def apply_matrix(pattern, owned_blocks, spectrum, sources, start, hamiltonian):
    columns, rows = sources[0].shape
    block_count, block_size, width = hamiltonian.shape
    reach_dev = len(sources) // 2
    first_apply = start is None
    scalar = pl.BlockSpec(memory_space=pltpu.SMEM)
    vector = pl.BlockSpec(memory_space=pltpu.VMEM)
    far = pl.BlockSpec(memory_space=pl.ANY)
    out = jax.ShapeDtypeStruct((columns, rows), jnp.float32)
    gram = jax.ShapeDtypeStruct((columns, columns), jnp.float32)
    operands = list(sources) + ([] if first_apply else [start])
    return pl.pallas_call(
        functools.partial(apply_kernel, first_apply, reach_dev),
        out_shape=out if first_apply else (out, gram),
        in_specs=[scalar] * 3 + [vector] * len(operands) + [far],
        out_specs=vector if first_apply else (vector, vector),
        scratch_shapes=[
            pltpu.VMEM((block_count, block_size, width), jnp.float32),
            pltpu.VMEM((len(sources) * rows, SPLITS * columns), jnp.bfloat16),
            pltpu.VMEM((rows, columns), jnp.float32),
            pltpu.SemaphoreType.DMA((block_count,)),
        ],
        compiler_params=pltpu.CompilerParams(vmem_limit_bytes=32 * 2**20),
        name="apply_first" if first_apply else "apply_second",
    )(pattern, owned_blocks, spectrum, *operands, hamiltonian)


def factor_kernel(total, gram_ref, flat_ref, basis_ref, upper_ref, spread_ref):
    columns = gram_ref.shape[0]
    tile = 8
    width = 2 * columns
    gram = gram_ref[...]
    row = lax.broadcasted_iota(jnp.int32, (columns, columns), 0)
    lane = lax.broadcasted_iota(jnp.int32, (columns, columns), 1)
    unit = (row == lane).astype(jnp.float32)
    whole = jnp.concatenate([gram, unit], axis=1)
    tiles = [whole[i * tile : (i + 1) * tile, :] for i in range(columns // tile)]
    place = lax.broadcasted_iota(jnp.int32, (tile, width), 0)
    for j in range(columns):
        home, inner = divmod(j, tile)
        pivot_row = tiles[home][inner : inner + 1, :]
        scaled = pivot_row / pivot_row[:, j : j + 1]
        for i in range(home, columns // tile):
            factor = jnp.broadcast_to(tiles[i][:, j : j + 1], (tile, width))
            if i == home:
                factor = jnp.where(place > inner, factor, 0.0)
            tiles[i] = tiles[i] - factor * scaled
    done = jnp.concatenate(tiles, axis=0)
    weighted = done[:, :columns]
    diagonal = jnp.sum(jnp.where(row == lane, weighted, 0.0), axis=1, keepdims=True)
    root = jnp.sqrt(diagonal)
    upper = jnp.where(row <= lane, weighted / root, 0.0)
    inverse = done[:, columns:] / root
    upper_ref[...] = upper / total
    size = jnp.sum(jnp.where(row == lane, gram, 0.0), axis=0, keepdims=True)
    spread_ref[...] = jnp.broadcast_to(jnp.sum(inverse * inverse * size), spread_ref.shape)
    ortho = jnp.dot(
        inverse,
        flat_ref[...],
        precision=lax.Precision.HIGHEST,
        preferred_element_type=jnp.float32,
    )
    basis_ref[...] = ortho * total


def factor(gram, flat, total):
    vector = pl.BlockSpec(memory_space=pltpu.VMEM)
    return pl.pallas_call(
        functools.partial(factor_kernel, total),
        out_shape=(
            jax.ShapeDtypeStruct(flat.shape, jnp.float32),
            jax.ShapeDtypeStruct(gram.shape, jnp.float32),
            jax.ShapeDtypeStruct((8, 128), jnp.float32),
        ),
        in_specs=[vector] * 2,
        out_specs=(vector,) * 3,
        name="factor",
    )(gram, flat)


def summed(values):
    for axis in reversed(AXES):
        size = lax.axis_size(axis)
        if size & (size - 1):
            values = lax.psum(values, axis)
            continue
        step = 1
        while step < size:
            route = [(i, i ^ step) for i in range(size)]
            values = values + lax.ppermute(values, axis, route)
            step *= 2
    return values


def on_device(block_vectors, hamiltonian, pattern, owned_blocks, spectrum):
    block_count = pattern.shape[0]
    block_size = hamiltonian.shape[1]
    rows = block_vectors.shape[0]
    reach_dev = (BAND + block_count - 1) // block_count
    total = float(rows * lax.axis_size(AXES)) ** 0.5

    def extended(values):
        route = [d for d in range(reach_dev, -reach_dev - 1, -1)]
        return [shifted(values, d) if d else values for d in route]

    live = jnp.arange(rows, dtype=jnp.int32) < owned_blocks[0] * block_size
    first_vec = jnp.where(live[None, :], block_vectors.T, 0.0)
    second_vec = apply_matrix(
        pattern, owned_blocks, spectrum, extended(first_vec), None, hamiltonian
    )
    third_vec, local_gram = apply_matrix(
        pattern, owned_blocks, spectrum, extended(second_vec), first_vec, hamiltonian
    )
    basis, upper, spread = factor(summed(local_gram), third_vec, total)

    def second_pass(basis, upper):
        local = jnp.dot(
            basis, basis.T, precision=lax.Precision.HIGHEST, preferred_element_type=jnp.float32
        )
        again, upper_again, _ = factor(summed(local), basis, total)
        return again, jnp.dot(upper_again, upper, precision=lax.Precision.HIGHEST)

    basis, upper = lax.cond(
        spread[0, 0] <= 8.0 * basis.shape[0], lambda b, u: (b, u), second_pass, basis, upper
    )
    return basis.T, upper


def solution(mesh):
    placed = (
        P(AXES, None),
        P(AXES, None, None),
        P(AXES, None),
        P(AXES),
        P(),
    )
    return jax.shard_map(
        on_device,
        mesh=mesh,
        in_specs=placed,
        out_specs=(P(AXES, None), P()),
        check_vma=False,
    )
```
